32 devices in a mesh: loop: 16 (over z, x, core), tok: 2 (over y).
Axes of the slice: x: 2, y: 2, z: 4, core: 2. Of those that a mesh axis runs over, the one named last changes fastest.
Arguments:
- features: bfloat16 [2048, 4096], P('loop', 'tok'), may hold values from -6 to 6
- expert_rows: int32 [2, 768], replicated, may hold values from 0 to 2047, as said below
- route_weight: float32 [2, 768], replicated, may hold values from 0.1 to 1
- gate_proj: bfloat16 [2, 4096, 14336], P(None, 'tok', 'loop'), may hold values from -0.09375 to 0.09375
- up_proj: bfloat16 [2, 4096, 14336], P(None, 'tok', 'loop'), may hold values from -0.09375 to 0.09375
- down_proj: bfloat16 [2, 14336, 4096], P(None, 'loop', 'tok'), may hold values from -0.046875 to 0.046875
- out_grad: bfloat16 [2048, 4096], P('loop', 'tok'), may hold values from -6 to 6
Outputs:
- mixed: bfloat16 [2048, 4096], P('loop', 'tok')
- feature_grad: bfloat16 [2048, 4096], P('loop', 'tok')
- gate_grad: bfloat16 [2, 4096, 14336], P(None, 'tok', 'loop')
- up_grad: bfloat16 [2, 4096, 14336], P(None, 'tok', 'loop')
- down_grad: bfloat16 [2, 14336, 4096], P(None, 'loop', 'tok')
The draws below stay inside these ranges and needn't reach their ends.
Inputs may be any that keep to these rules, and one draw needn't show every extreme that they name: `expert_rows`: each expert's list holds 768 distinct tokens in ascending order, and tokens 0 and 2047 are in every list. Of the 128 tokens t with the same t // 128, at most 96 are in one list, and in every list exactly 96 come from one such index.
All inputs are finite; a program needn't handle non-finite values.
Results may differ from the reference program's by a relative error of at most 0.0049.
Values may be sent and summed in bfloat16 or wider, within the bound.
No kernel may reach another device: no remote copies, remote signals or barrier semaphores. Data moves between devices by JAX's collectives and lax.ppermute only.
A program may use at most 192 MiB of HBM per device.

```python
import math
import jax
import jax.numpy as jnp

D = 4096
FF = 14336
EXPERTS = 2
TOK_LOOP = 128
ROWS_E = 768
TOKENS = 2048


def draw_expert_rows(key, part):
    loops = TOKENS // TOK_LOOP
    average = ROWS_E // loops
    half = loops // 2
    lists = []
    for expert in range(EXPERTS):
        base = jax.random.fold_in(key, 101 + expert)
        key_shift, key_order, key_place, key_rank = jax.random.split(base, 4)
        shifts = jax.random.randint(key_shift, (half,), 0, average).at[0].set(average)
        counts = average + jnp.concatenate([shifts, -shifts])
        counts = counts[jax.random.permutation(key_order, loops)]
        empty_at = jnp.argmin(counts)
        target = jax.random.randint(key_place, (), 1, loops - 1)
        counts = jnp.roll(counts, target - empty_at)
        scores = jax.random.randint(key_rank, (loops, TOK_LOOP), 0, 1 << 20) * TOK_LOOP + jnp.arange(TOK_LOOP)[None, :]
        scores = scores.at[0, 0].set(-1).at[loops - 1, TOK_LOOP - 1].set(-1)
        ranks = jnp.argsort(jnp.argsort(scores, axis=1), axis=1)
        chosen = (ranks < counts[:, None]).reshape(-1)
        order_key = jnp.where(chosen, 0, TOKENS) + jnp.arange(TOKENS)
        lists.append(jnp.argsort(order_key)[:ROWS_E].astype(jnp.int32))
    return jnp.stack(lists)


def block_scale(key, extent, cuts, least, top_value):
    factor_of = 1.0
    for dim, parts in cuts:
        steps = jax.random.uniform(jax.random.fold_in(jax.random.fold_in(key, 6), dim), (parts,), jnp.float32, least / len(cuts), top_value / len(cuts))
        factor_of = factor_of * jnp.repeat(jnp.exp(steps), extent[dim] // parts).reshape((-1,) + (1,) * (len(extent) - 1 - dim))
    return factor_of


def centred(key, shape, spread, bound, shards=(), held_as=jnp.bfloat16):
    drawn = spread * jax.random.normal(key, shape, jnp.float32)
    if shards:
        drawn = drawn * block_scale(key, shape, shards, -0.22, 0.18)
    return jnp.clip(drawn, -bound, bound).astype(held_as)


def setup_inputs(seed: int = 0) -> dict:
    keys = jax.random.split(jax.random.key(seed), 8)
    features = centred(keys[0], (TOKENS, D), 1.0, 6.0, ((0, 16), (1, 2)))
    expert_rows = draw_expert_rows(jax.random.fold_in(keys[7], 71), 0)
    route_weight = jnp.clip(jnp.exp(jax.random.uniform(keys[2], (EXPERTS, ROWS_E), jnp.float32, math.log(0.1), math.log(1.0))), 0.1, 1.0)
    gate_proj = centred(keys[3], (EXPERTS, D, FF), D ** -0.5, 0.09375, ((1, 2), (2, 16)))
    up_proj = centred(keys[4], (EXPERTS, D, FF), D ** -0.5, 0.09375, ((1, 2), (2, 16)))
    down_proj = centred(keys[5], (EXPERTS, FF, D), FF ** -0.5, 0.046875, ((1, 16), (2, 2)))
    out_grad = centred(keys[6], (TOKENS, D), 1.0, 6.0, ((0, 16), (1, 2)))
    return {"features": features, "expert_rows": expert_rows, "route_weight": route_weight, "gate_proj": gate_proj, "up_proj": up_proj, "down_proj": down_proj, "out_grad": out_grad}


def reference(features, expert_rows, route_weight, gate_proj, up_proj, down_proj, out_grad):
    token_rows = features[expert_rows].astype(jnp.float32)
    grad_rows = out_grad[expert_rows].astype(jnp.float32)
    flat_rows = expert_rows.reshape(-1)
    gate = jnp.einsum("erd,edf->erf", token_rows, gate_proj.astype(jnp.float32))
    upval = jnp.einsum("erd,edf->erf", token_rows, up_proj.astype(jnp.float32))
    back = jnp.einsum("erd,efd->erf", grad_rows, down_proj.astype(jnp.float32))
    weights = route_weight[:, :, None]
    scaled = (weights * jax.nn.silu(gate) * upval).astype(jnp.bfloat16)
    scaled_wide = scaled.astype(jnp.float32)
    sigma = jax.nn.sigmoid(gate)
    weighted = weights * back
    gate_bar = (weighted * upval * sigma * (1.0 + gate * (1.0 - sigma))).astype(jnp.bfloat16)
    up_bar = (weighted * gate * sigma).astype(jnp.bfloat16)
    gate_bar_wide = gate_bar.astype(jnp.float32)
    up_bar_wide = up_bar.astype(jnp.float32)
    term = jnp.einsum("erf,efd->erd", scaled_wide, down_proj.astype(jnp.float32))
    mixed = jnp.zeros((TOKENS, D), jnp.float32).at[flat_rows].add(term.reshape(-1, D))
    input_term = jnp.einsum("erf,edf->erd", gate_bar_wide, gate_proj.astype(jnp.float32))
    input_term = input_term + jnp.einsum("erf,edf->erd", up_bar_wide, up_proj.astype(jnp.float32))
    feature_grad = jnp.zeros((TOKENS, D), jnp.float32).at[flat_rows].add(input_term.reshape(-1, D))
    gate_grad = jnp.einsum("erd,erf->edf", token_rows, gate_bar_wide).astype(jnp.bfloat16)
    up_grad = jnp.einsum("erd,erf->edf", token_rows, up_bar_wide).astype(jnp.bfloat16)
    down_grad = jnp.einsum("erf,erd->efd", scaled_wide, grad_rows).astype(jnp.bfloat16)
    return (mixed.astype(jnp.bfloat16), feature_grad.astype(jnp.bfloat16), gate_grad, up_grad, down_grad)
```

```python
import functools

import jax
import jax.numpy as jnp
import numpy as np
from jax import lax
from jax.experimental import pallas as pl
from jax.experimental.pallas import tpu as pltpu
from jax.sharding import PartitionSpec as P

BF16 = jnp.bfloat16
F32 = jnp.float32
VMEM_LIMIT = 56 * 1024 * 1024
ROW_TILE = 256
TOKEN_TILE = 256
HIDDEN_TILE = 256


ORDER = (
    ("pick", "token", 0),
    ("part", "gate", 0),
    ("part", "up", 0),
    ("pick", "token", 1),
    ("pair", 1),
    ("pick", "grad", 0),
    ("part", "back", 0),
    ("hidden", "mixed", 0),
    ("pick", "grad", 1),
    ("part", "back", 1),
    ("weigh", "down", 0),
    ("hidden", "mixed", 1),
    ("weigh", "down", 1),
    ("across", "mixed"),
    ("hidden", "grad", 0),
    ("onward", "mixed", 0),
    ("weigh", "gate", 0),
    ("onward", "mixed", 1),
    ("weigh", "up", 0),
    ("hidden", "grad", 1),
    ("finish", "mixed"),
    ("across", "grad"),
    ("weigh", "gate", 1),
    ("onward", "grad", 0),
    ("weigh", "up", 1),
    ("onward", "grad", 1),
    ("finish", "grad"),
)


COST = pl.CostEstimate(flops=40_000_000_000, bytes_accessed=1024, transcendentals=0)


def params():
    return pltpu.CompilerParams(vmem_limit_bytes=VMEM_LIMIT)


def resident(shape, index):
    return pl.BlockSpec(shape, index, pipeline_mode=pl.Buffered(1))


def after_specs(after):
    return [pl.BlockSpec(memory_space=pl.ANY)] * len(after)


def pair_kernel(a_ref, gate_ref, up_ref, *refs):
    wide_ref, sent_ref = refs[-2:]

    def product(weight_ref):
        out = jnp.dot(a_ref[...], weight_ref[...], preferred_element_type=F32)
        wide_ref[...] = out
        sent_ref[...] = out.astype(BF16)

    pl.when(pl.program_id(1) == 0)(lambda: product(gate_ref))
    pl.when(pl.program_id(1) == 1)(lambda: product(up_ref))


def pair_product(rows, gate, up, expert, after):
    count, depth = rows.shape
    hidden = gate.shape[2]
    tile = count // 3
    weight_spec = resident((None, depth, hidden), lambda i, j: (expert, 0, 0))
    return pl.pallas_call(
        pair_kernel,
        grid=(3, 2),
        in_specs=[pl.BlockSpec((tile, depth), lambda i, j: (i, 0)), weight_spec, weight_spec]
        + after_specs(after),
        out_specs=[pl.BlockSpec((None, tile, hidden), lambda i, j: (j, i, 0))] * 2,
        out_shape=[
            jax.ShapeDtypeStruct((2, count, hidden), F32),
            jax.ShapeDtypeStruct((2, count, hidden), BF16),
        ],
        compiler_params=params(),
        cost_estimate=COST,
    )(rows, gate, up, *after)


def order_kernel(block, column_ref, line_ref, weight_ref, rows_out, weights_out, both_out):
    def keys(tokens, both, expert):
        late = both if expert == 0 else 1.0 - both
        held = lax.div(tokens, block)
        return (held * 2 * block + (tokens - held * block)).astype(F32) + late * block

    for e in range(2):
        column, line = column_ref[e], line_ref[e]
        both_column = jnp.max((column == line_ref[1 - e]).astype(F32), axis=1, keepdims=True)
        both_line = jnp.max((line == column_ref[1 - e]).astype(F32), axis=0, keepdims=True)
        before = keys(column, both_column, e) < keys(line, both_line, e)
        place = jnp.sum(before.astype(F32), axis=0, keepdims=True)
        spot = lax.broadcasted_iota(jnp.int32, column.shape, 0).astype(F32)
        chosen = (place == spot).astype(F32)
        rows = jnp.sum(chosen * line.astype(F32), axis=1, keepdims=True)
        rows_out[e] = rows.astype(jnp.int32)
        weights_out[e] = jnp.sum(chosen * weight_ref[e], axis=1, keepdims=True)
        both_out[e] = both_line


def order_rows(expert_rows, route_weight, block):
    experts, count = expert_rows.shape
    return pl.pallas_call(
        functools.partial(order_kernel, block),
        out_shape=[
            jax.ShapeDtypeStruct((experts, count, 1), jnp.int32),
            jax.ShapeDtypeStruct((experts, count, 1), F32),
            jax.ShapeDtypeStruct((experts, 1, count), F32),
        ],
        compiler_params=params(),
    )(expert_rows[:, :, None], expert_rows[:, None, :], route_weight[:, None, :])


def pick_kernel(first_ref, last_ref, rows_ref, table_ref, *refs):
    out_ref, acc = refs[-2:]
    i = pl.program_id(0)
    rows = rows_ref[...]
    acc[...] = jnp.zeros_like(acc)
    lane = lax.broadcasted_iota(jnp.int32, (rows.shape[0], TOKEN_TILE), 1)

    def step(b, carry):
        base = pl.multiple_of(b * TOKEN_TILE, TOKEN_TILE)
        hot = (lane + base == rows).astype(F32).astype(BF16)
        acc[...] += jnp.dot(
            hot, table_ref[pl.ds(base, TOKEN_TILE), :], preferred_element_type=F32
        )
        return carry

    lax.fori_loop(first_ref[i], last_ref[i] + 1, step, 0)
    out_ref[...] = acc[...].astype(BF16)


def pick_rows(table, rows, after):
    count = rows.shape[0]
    tokens, width = table.shape
    tiles = count // ROW_TILE
    tiled = rows.reshape(tiles, ROW_TILE) // TOKEN_TILE
    return pl.pallas_call(
        pick_kernel,
        grid_spec=pltpu.PrefetchScalarGridSpec(
            num_scalar_prefetch=2,
            grid=(tiles,),
            in_specs=[
                pl.BlockSpec((ROW_TILE, 1), lambda i, *_: (i, 0)),
                resident((tokens, width), lambda i, *_: (0, 0)),
            ]
            + after_specs(after),
            out_specs=pl.BlockSpec((ROW_TILE, width), lambda i, *_: (i, 0)),
            scratch_shapes=[pltpu.VMEM((ROW_TILE, width), F32)],
        ),
        out_shape=jax.ShapeDtypeStruct((count, width), BF16),
        compiler_params=params(),
        cost_estimate=COST,
    )(tiled[:, 0], tiled[:, -1], rows, table, *after)


def part_kernel(flip, a_ref, w_ref, *refs):
    wide_ref, sent_ref = refs[-2:]
    dims = (((1,), (1 if flip else 0,)), ((), ()))
    out = lax.dot_general(a_ref[...], w_ref[...], dims, preferred_element_type=F32)
    wide_ref[...] = out
    sent_ref[...] = out.astype(BF16)


def partial_product(rows, weight, expert, flip, after):
    count, depth = rows.shape
    hidden = weight.shape[1] if flip else weight.shape[2]
    tile = count // 3
    return pl.pallas_call(
        functools.partial(part_kernel, flip),
        grid=(3,),
        in_specs=[
            pl.BlockSpec((tile, depth), lambda i: (i, 0)),
            resident((None,) + weight.shape[1:], lambda i: (expert, 0, 0)),
        ]
        + after_specs(after),
        out_specs=[
            pl.BlockSpec((tile, hidden), lambda i: (i, 0)),
            pl.BlockSpec((tile, hidden), lambda i: (i, 0)),
        ],
        out_shape=[
            jax.ShapeDtypeStruct((count, hidden), F32),
            jax.ShapeDtypeStruct((count, hidden), BF16),
        ],
        compiler_params=params(),
        cost_estimate=COST,
    )(rows, weight, *after)


def hidden_kernel(backward, cap, layout_ref, weight_ref, *refs):
    shares = 6 if backward else 4
    terms = 2 if backward else 1
    parts, rights = refs[:shares], refs[shares : shares + terms]
    merge = layout_ref is not None
    first, acc = (refs[shares + terms], refs[-1]) if merge else (None, None)
    outs = refs[-(5 + terms) : -1] if merge else refs[-(1 + terms) :]
    lefts, results = outs[:terms], outs[terms:]
    count = lefts[0].shape[0]
    step = pl.program_id(0)
    chunks = count // HIDDEN_TILE

    @pl.when(step < chunks)
    def _():
        at = pl.ds(pl.multiple_of(step * HIDDEN_TILE, HIDDEN_TILE), HIDDEN_TILE)
        gate = parts[0][...] + parts[1][...].astype(F32)
        upval = parts[2][...] + parts[3][...].astype(F32)
        weights = weight_ref[...]
        sigma = jax.nn.sigmoid(gate)
        if backward:
            weighted = weights * (parts[4][...] + parts[5][...].astype(F32))
            gate_bar = weighted * upval * sigma * (1.0 + gate * (1.0 - sigma))
            lefts[0][at, :] = gate_bar.astype(BF16)
            lefts[1][at, :] = (weighted * gate * sigma).astype(BF16)
        else:
            lefts[0][at, :] = (weights * (gate * sigma) * upval).astype(BF16)

    @pl.when(step >= chunks)
    def _():
        dims = (((1,), (1 if backward else 0,)), ((), ()))
        total = None
        for left, right in zip(lefts, rights):
            term = lax.dot_general(left[...], right[...], dims, preferred_element_type=F32)
            total = term if total is None else total + term
        if not merge:
            results[0][pl.ds(0, count), :] = total
            return
        blocks, block = results[0].shape[:2]
        acc[pl.ds(block, count), :] = total
        slot = lax.broadcasted_iota(jnp.int32, (block, total.shape[1]), 0)
        near = slot[:cap]

        def run(ref, start, length):
            base = pl.multiple_of((start // 8) * 8, 8)
            window = ref[pl.ds(base, length + 8), :]
            return pltpu.roll(window, length + 8 - (start - base), 0)[:length]

        for which in range(4):
            for z in range(blocks):
                start0, count0, start1, lead, count1 = (
                    layout_ref[i, which * blocks + z] for i in range(5)
                )
                rows1 = run(acc, block + start1 - lead, block)
                rows1 = jnp.where((slot >= lead) & (slot < lead + count1), rows1, 0.0)
                rows0 = jnp.where(near < count0, run(first, start0, cap), 0.0)
                results[which][z, pl.ds(0, cap), :] = (rows0 + rows1[:cap]).astype(BF16)
                results[which][z, pl.ds(cap, block - cap), :] = rows1[cap:].astype(BF16)


def hidden_rows(backward, weights, shares, rights, expert, first, layout, block, cap, after):
    places = [place for _, place in shares]
    shares = [share for share, _ in shares]
    count, hidden = shares[0].shape[-2:]
    width = rights[0].shape[1] if backward else rights[0].shape[2]
    tile = min(512, width)
    terms = len(rights)
    chunks = count // HIDDEN_TILE
    padded = count + cap + 16

    def early(i, *_):
        return (jnp.minimum(i, chunks - 1), 0)

    def late(i):
        return jnp.maximum(i - chunks, 0)

    if backward:
        right_spec = pl.BlockSpec((None, tile, hidden), lambda i, *_: (expert, late(i), 0))
    else:
        right_spec = pl.BlockSpec((None, hidden, tile), lambda i, *_: (expert, 0, late(i)))
    rows_spec = pl.BlockSpec((padded, tile), lambda i, *_: (0, late(i)))
    in_specs = [pl.BlockSpec((HIDDEN_TILE, 1), early)]
    for place in places:
        if place is None:
            in_specs.append(pl.BlockSpec((HIDDEN_TILE, hidden), early))
        else:
            index = functools.partial(lambda place, i, *_: (place,) + early(i), place)
            in_specs.append(pl.BlockSpec((None, HIDDEN_TILE, hidden), index))
    in_specs += [right_spec] * terms
    out_specs = [resident((count, hidden), lambda i, *_: (0, 0))] * terms
    out_shape = [jax.ShapeDtypeStruct((count, hidden), BF16)] * terms
    kernel = functools.partial(hidden_kernel, backward, cap)
    if first is None:
        out_specs += [rows_spec]
        out_shape += [jax.ShapeDtypeStruct((padded, width), F32)]
        kernel = functools.partial(kernel, None)
        scratch, extra, scalars = [], [], []
    else:
        blocks = layout.shape[1] // 4
        in_specs += [rows_spec]
        out_specs += [pl.BlockSpec((blocks, block, tile), lambda i, *_: (0, 0, late(i)))] * 4
        out_shape += [jax.ShapeDtypeStruct((blocks, block, width), BF16)] * 4
        scratch = [pltpu.VMEM((block + count + block + 8, tile), F32)]
        extra, scalars = [first], [layout]
    outs = pl.pallas_call(
        kernel,
        grid_spec=pltpu.PrefetchScalarGridSpec(
            num_scalar_prefetch=len(scalars),
            grid=(chunks + width // tile,),
            in_specs=in_specs + after_specs(after),
            out_specs=out_specs,
            scratch_shapes=scratch,
        ),
        out_shape=out_shape,
        compiler_params=params(),
        cost_estimate=COST,
    )(*scalars, weights, *shares, *rights, *extra, *after)
    return outs[:terms], outs[terms:]


def grad_kernel(left_ref, right_ref, *refs):
    refs[-1][...] = lax.dot_general(
        left_ref[...], right_ref[...], (((0,), (0,)), ((), ())), preferred_element_type=F32
    ).astype(BF16)


def weight_grad(left, right, expert, experts, earlier, after):
    count, rows = left.shape
    columns = right.shape[1]
    tile = next(t for t in (512, 448, 128, rows) if rows % t == 0 and (t % 128 == 0 or t == rows))
    extra = ([] if earlier is None else [earlier]) + list(after)
    return pl.pallas_call(
        grad_kernel,
        grid=(rows // tile,),
        in_specs=[
            pl.BlockSpec((count, tile), lambda i: (0, i)),
            resident((count, columns), lambda i: (0, 0)),
        ]
        + after_specs(extra),
        out_specs=pl.BlockSpec((None, tile, columns), lambda i: (expert, i, 0)),
        out_shape=jax.ShapeDtypeStruct((experts, rows, columns), BF16),
        input_output_aliases={} if earlier is None else {2: 0},
        compiler_params=params(),
        cost_estimate=COST,
    )(left, right, *extra)


class Ring:
    def __init__(self, size):
        self.size = size
        self.depth = size // 4
        self.index = lax.axis_index("loop")
        self.z = self.index // 4
        self.x = (self.index // 2) % 2
        self.core = self.index % 2

    def send(self, value, dz=0, flip_x=False, flip_core=False):
        pairs = []
        for i in range(self.size):
            z, x, c = i // 4, (i // 2) % 2, i % 2
            z = (z + dz) % self.depth
            pairs.append((i, (z * 2 + (x ^ flip_x)) * 2 + (c ^ flip_core)))
        return lax.ppermute(value, "loop", pairs)

    def owners(self):
        z = (self.z + 1 + np.arange(self.depth)) % self.depth
        return jnp.concatenate(
            [(z * 2 + (self.x ^ x)) * 2 + (self.core ^ c) for c in (0, 1) for x in (0, 1)]
        )


def sum_kernel(sums, stacks, *refs):
    ins, outs = refs[:stacks], refs[-len(sums) :]
    for out, blocks in zip(outs, sums):
        for place, terms in enumerate(blocks):
            total = None
            for which, index in terms:
                term = ins[which][index].astype(F32)
                total = term if total is None else total + term
            out[place] = total.astype(BF16)


def sum_blocks(stacks, sums, after):
    rows, width = stacks[0].shape[1:]
    tile = min(1024, width)

    def spec(blocks):
        return pl.BlockSpec((blocks, rows, tile), lambda i: (0, 0, i))

    return pl.pallas_call(
        functools.partial(sum_kernel, sums, len(stacks)),
        grid=(width // tile,),
        in_specs=[spec(t.shape[0]) for t in stacks] + after_specs(after),
        out_specs=[spec(len(blocks)) for blocks in sums],
        out_shape=[jax.ShapeDtypeStruct((len(blocks), rows, width), BF16) for blocks in sums],
        compiler_params=params(),
        cost_estimate=COST,
    )(*stacks, *after)


def place_kernel(terms, hot_ref, *refs):
    total = None
    for ref in refs[:terms]:
        term = ref[0].astype(F32)
        total = term if total is None else total + term
    out = jnp.dot(
        hot_ref[...], total, precision=lax.Precision.HIGHEST, preferred_element_type=F32
    )
    refs[-1][...] = out.astype(BF16)


def place_slots(hot, stacks, after):
    block = hot.shape[0]
    width = stacks[0].shape[2]
    tile = min(512, width)
    specs = [
        pl.BlockSpec((1, block, tile), functools.partial(lambda last, i: (last, 0, i), t.shape[0] - 1))
        for t in stacks
    ]
    return pl.pallas_call(
        functools.partial(place_kernel, len(stacks)),
        grid=(width // tile,),
        in_specs=[pl.BlockSpec((block, block), lambda i: (0, 0))] + specs + after_specs(after),
        out_specs=pl.BlockSpec((block, tile), lambda i: (0, i)),
        out_shape=jax.ShapeDtypeStruct((block, width), BF16),
        compiler_params=params(),
        cost_estimate=COST,
    )(hot, *stacks, *after)


class Reduction:
    def __init__(self, ring, held):
        self.ring, self.held = ring, held
        self.got_far = ring.send(held[3], flip_core=True)
        self.got_near = ring.send(held[2], flip_core=True)
        depth = ring.depth
        turns = sorted(range(1, depth), key=lambda k: (-min(k, depth - k), k))
        cut = max(1, (depth - 1) // 3)
        self.groups = [turns[:cut], turns[cut:], [depth]]

    def across(self, after):
        sums = [[[(0, k - 1), (1, k - 1)] for k in group] for group in self.groups]
        values = sum_blocks([self.held[1], self.got_far], sums, after)
        self.from_x = [self.ring.send(value, flip_x=True) for value in values]
        self.along = []
        return values[0]

    def onward(self, turn, after):
        group = self.groups[turn]
        sums = [[[(0, k - 1), (1, k - 1), (2, place)]] for place, k in enumerate(group)]
        values = sum_blocks([self.held[0], self.got_near, self.from_x[turn]], sums, after)
        self.along += [self.ring.send(value, dz=k) for value, k in zip(values, group)]
        return values[0]

    def finish(self, hot, after):
        stacks = [self.held[0], self.got_near, self.from_x[2]] + self.along
        return place_slots(hot, stacks, after)


def over_tok(wide, sent):
    if lax.axis_size("tok") == 2:
        return [wide, lax.ppermute(sent, "tok", [(0, 1), (1, 0)])]
    return [lax.psum(wide, "tok"), jnp.zeros_like(sent)]


def local(features, expert_rows, route_weight, gate_proj, up_proj, down_proj, out_grad):
    loop_size = lax.axis_size("loop")
    ring = Ring(loop_size)
    block = features.shape[0]
    experts, rows_each = expert_rows.shape
    cap = 2 * rows_each // loop_size
    token_table = lax.all_gather(features, "loop", axis=0, tiled=True)
    grad_table = lax.all_gather(out_grad, "loop", axis=0, tiled=True)

    ordered, weights, both = order_rows(expert_rows, route_weight, block)
    edges = jnp.arange(loop_size + 1, dtype=jnp.int32) * block
    bounds = jnp.sum((expert_rows[:, None, :] < edges[None, :, None]).astype(jnp.int32), axis=2)
    starts, counts = bounds[:, :-1], bounds[:, 1:] - bounds[:, :-1]
    alone = (both[0, 0] < 0.5) & (expert_rows[0] // block == jnp.arange(loop_size)[:, None])
    lead = jnp.sum(alone.astype(jnp.int32), axis=1)
    layout = jnp.stack([starts[0], counts[0], starts[1], lead, counts[1]])
    start0, count0, start1, first1, count1 = jnp.take(layout, ring.index, axis=1)
    layout = jnp.take(layout, ring.owners(), axis=1)
    slot = jnp.arange(block, dtype=jnp.int32)

    def token_at(e, row):
        return jnp.take(ordered[e, :, 0], jnp.clip(row, 0, rows_each - 1))

    late = (slot >= first1) & (slot < first1 + count1)
    token = jnp.where(late, token_at(1, start1 + slot - first1), -1)
    token = jnp.where(slot < count0, token_at(0, start0 + slot), token)
    hot = (ring.index * block + slot)[:, None] == token[None, :]
    hot = hot.astype(F32)

    rows = {"token": [None, None], "grad": [None, None]}
    shares = {"gate": [None, None], "up": [None, None], "back": [None, None]}
    lefts = {"mixed": [None, None], "grad": [None, None]}
    first, sums, placed = {}, {}, {}
    grads = {"gate": None, "up": None, "down": None}
    last = []

    def pick(which, e):
        table = token_table if which == "token" else grad_table
        rows[which][e] = pick_rows(table, ordered[e], last)
        return rows[which][e]

    def part(which, e):
        source = rows["grad" if which == "back" else "token"][e]
        weight = {"gate": gate_proj, "up": up_proj, "back": down_proj}[which]
        share = partial_product(source, weight, e, which == "back", last)
        shares[which][e] = [(value, None) for value in over_tok(*share)]
        return share[0]

    def pair(e):
        share = pair_product(rows["token"][e], gate_proj, up_proj, e, last)
        both_shares = over_tok(*share)
        for place, which in enumerate(("gate", "up")):
            shares[which][e] = [(value, place) for value in both_shares]
        return share[0]

    def hidden(which, e):
        backward = which == "grad"
        parts = shares["gate"][e] + shares["up"][e] + (shares["back"][e] if backward else [])
        rights = [gate_proj, up_proj] if backward else [down_proj]
        lefts[which][e], results = hidden_rows(
            backward, weights[e], parts, rights, e, first.get(which), layout, block, cap, last
        )
        if e:
            sums[which] = Reduction(ring, results)
        else:
            first[which] = results[0]
        return lefts[which][e][0]

    def across(which):
        return sums[which].across(last)

    def onward(which, turn):
        return sums[which].onward(turn, last)

    def finish(which):
        placed[which] = sums[which].finish(hot, last)
        return placed[which]

    def weigh(which, e):
        if which == "down":
            left, right = lefts["mixed"][e][0], rows["grad"][e]
        else:
            left, right = rows["token"][e], lefts["grad"][e][0 if which == "gate" else 1]
        grads[which] = weight_grad(left, right, e, experts, grads[which], last)
        return grads[which]

    steps = {
        "pick": pick,
        "part": part,
        "pair": pair,
        "hidden": hidden,
        "across": across,
        "onward": onward,
        "finish": finish,
        "weigh": weigh,
    }
    for step, *detail in ORDER:
        last = [steps[step](*detail)]
    return (placed["mixed"], placed["grad"], grads["gate"], grads["up"], grads["down"])


def solution(mesh):
    placed = (
        P("loop", "tok"),
        P(),
        P(),
        P(None, "tok", "loop"),
        P(None, "tok", "loop"),
        P(None, "loop", "tok"),
        P("loop", "tok"),
    )
    return jax.shard_map(
        local,
        mesh=mesh,
        in_specs=placed,
        out_specs=(
            P("loop", "tok"),
            P("loop", "tok"),
            P(None, "tok", "loop"),
            P(None, "tok", "loop"),
            P(None, "loop", "tok"),
        ),
        check_vma=False,
    )
```
